32 devices in a mesh: row: 4 (over z), col: 8 (over y, x, core).
Axes of the slice: x: 2, y: 2, z: 4, core: 2. Of those that a mesh axis runs over, the one named last changes fastest.
Arguments:
- embeds: bfloat16 [6144, 768], P('col'), may hold values from -6 to 6
- labels: bfloat16 [6144, 1000], P('col'), may hold values from -6 to 6
- sharpness: float32 [6144], P('col'), may hold values from 0.5 to 100
- pattern: int32 [48, 16], P('col'), may hold values from 0 to 47, as said below
- mask_pos: int32 [6144, 50], P('col'), may hold values from 0 to 2047, as said below
Outputs:
- propagated: bfloat16 [6144, 1000], P('col', 'row')
The draws below stay inside these ranges and needn't reach their ends.
Inputs may be any that keep to these rules, and one draw needn't show every extreme that they name: `pattern`: split the row blocks into runs of 6 and the slots into runs of 4; within one run of row blocks and one run of slots, ids that lie in the same run of 6 block ids are equal. `mask_pos`: the 50 positions of a row are distinct; position k * 128 + m names row m of the row block's k-th candidate block.
All inputs are finite; a program needn't handle non-finite values.
Results may differ from the reference program's by a relative error of at most 0.012.
Values may be sent and summed in bfloat16 or wider, within the bound.
A program may use at most 128 MiB of HBM per device.

```python
import math
import jax
import jax.numpy as jnp
from jax import lax

D = 768
C = 1000
BLOCK = 128
SLOTS = 16
NEIGHBOURS = 50
CANDIDATES = 2048
ROWS = 6144
BLOCKS = 48
BLOCKS_COL = 6
SLOTS_DEV = 4


def draw_sharpness(key, part):
    first_key = jax.random.fold_in(jax.random.fold_in(key, 3), 0)
    base = jnp.exp(jax.random.uniform(first_key, (ROWS,), jnp.float32, math.log(0.5), math.log(4.0)))
    return base.astype(jnp.float32)


def draw_pattern(key, part):
    col_count = BLOCKS // BLOCKS_COL
    row_count = SLOTS // SLOTS_DEV
    keys = jax.random.split(jax.random.fold_in(key, 11), 4)
    chosen = jax.random.randint(keys[0], (col_count, row_count, col_count), 0, BLOCKS_COL)
    first_draw = jax.random.randint(keys[1], (BLOCKS, SLOTS), 0, col_count)
    second_draw = jax.random.randint(keys[2], (BLOCKS, SLOTS), 0, col_count)
    hubs = jax.random.permutation(keys[3], col_count)
    owners = hubs[jnp.minimum(first_draw, second_draw)]
    col_group = (jnp.arange(BLOCKS, dtype=jnp.int32) // BLOCKS_COL)[:, None]
    row_group = (jnp.arange(SLOTS, dtype=jnp.int32) // SLOTS_DEV)[None, :]
    local_ids = chosen[col_group, row_group, owners]
    return (owners * BLOCKS_COL + local_ids).astype(jnp.int32)


def draw_mask_pos(key, part):
    first_key, second_key = jax.random.split(jax.random.fold_in(key, 23), 2)
    stride = CANDIDATES // NEIGHBOURS
    jitter = jax.random.randint(first_key, (ROWS, NEIGHBOURS), 0, stride)
    offset = jax.random.randint(second_key, (ROWS, 1), 0, CANDIDATES)
    steps_base = jnp.arange(NEIGHBOURS, dtype=jnp.int32)[None, :] * stride
    return ((steps_base + jitter + offset) % CANDIDATES).astype(jnp.int32)


def steps_of(key, shape, cuts, least, largest):
    def one(position, shards_of):
        heights = jax.random.uniform(jax.random.fold_in(jax.random.fold_in(key, 6), position), (shards_of,), jnp.float32, least / len(cuts), largest / len(cuts))
        return jnp.repeat(jnp.exp(heights), shape[position] // shards_of).reshape((-1,) + (1,) * (len(shape) - position - 1))

    level = one(*cuts[0])
    for cut in cuts[1:]:
        level = level * one(*cut)
    return level


def scatter_about(key, dims, scale, bound, shards=(), kind=jnp.bfloat16):
    values = jax.random.normal(key, dims, jnp.float32) * scale
    if len(shards) > 0:
        values = steps_of(key, dims, shards, -0.22, 0.18) * values
    return jnp.clip(values, min=-bound, max=bound).astype(kind)


def setup_inputs(seed: int = 0) -> dict:
    arg_keys = jax.random.split(jax.random.key(seed), 6)
    return {
        "embeds": scatter_about(arg_keys[0], (ROWS, D), 1.0, 6.0, ((0, 8),)),
        "labels": scatter_about(arg_keys[1], (ROWS, C), 1.0, 6.0, ((0, 8),)),
        "sharpness": draw_sharpness(jax.random.fold_in(arg_keys[5], 71), 0),
        "pattern": draw_pattern(jax.random.fold_in(arg_keys[5], 71), 0),
        "mask_pos": draw_mask_pos(jax.random.fold_in(arg_keys[5], 71), 0),
    }


mixing = 0.75

def block_weights(query, candidate_ids, sharp, positions):
    scores = jnp.dot(query, candidate_ids.T, preferred_element_type=jnp.float32) / math.sqrt(D)
    logits = scores * sharp[:, None]
    row_ids = jnp.arange(BLOCK, dtype=jnp.int32)[:, None]
    in_mask = jnp.zeros((BLOCK, CANDIDATES), jnp.float32).at[row_ids, positions].set(1.0) > 0.5
    top = lax.optimization_barrier(jnp.max(jnp.where(in_mask, logits, -jnp.inf), axis=1, keepdims=True))
    expo = jnp.where(in_mask, jnp.exp(logits - top), 0.0)
    totals = lax.optimization_barrier(jnp.sum(expo, axis=1, keepdims=True))
    return (expo / totals).astype(jnp.bfloat16)

def blend_label_block(weight_matrix, cand_labels, seed_rows):
    groups = SLOTS // SLOTS_DEV
    wide_w = weight_matrix.astype(jnp.float32).reshape(BLOCK, groups, SLOTS_DEV * BLOCK)
    wide_y = cand_labels.astype(jnp.float32).reshape(groups, SLOTS_DEV * BLOCK, C)
    pieces = jnp.einsum('qgk,gkc->gqc', wide_w, wide_y).astype(jnp.bfloat16)
    pieces = lax.optimization_barrier(pieces)
    summed = lax.optimization_barrier(jnp.sum(pieces.astype(jnp.float32), axis=0))
    return (mixing * summed + (1.0 - mixing) * seed_rows.astype(jnp.float32)).astype(jnp.bfloat16)

def reference(embeds, labels, sharpness, pattern, mask_pos):
    embedding_tiles = embeds.reshape(BLOCKS, BLOCK, D)
    lab_blocks = labels.reshape(BLOCKS, BLOCK, C)
    sharp_blocks = sharpness.reshape(BLOCKS, BLOCK)
    pos_blocks = mask_pos.reshape(BLOCKS, BLOCK, NEIGHBOURS)

    def first_round(index):
        ids = pattern[index]
        candidate_ids = embedding_tiles[ids].reshape(CANDIDATES, D)
        weight_matrix = block_weights(embedding_tiles[index], candidate_ids, sharp_blocks[index], pos_blocks[index])
        spread_rows = blend_label_block(weight_matrix, lab_blocks[ids], lab_blocks[index])
        return (weight_matrix, spread_rows)
    weight_matrix, spread = lax.map(first_round, jnp.arange(BLOCKS, dtype=jnp.int32))

    def second_round(index):
        return blend_label_block(weight_matrix[index], spread[pattern[index]], lab_blocks[index])
    result = lax.map(second_round, jnp.arange(BLOCKS, dtype=jnp.int32))
    return result.reshape(ROWS, C)
```

```python
import functools
import math

import jax
import jax.numpy as jnp
from jax import lax
from jax.experimental import pallas as pl
from jax.experimental.pallas import tpu as pltpu
from jax.sharding import PartitionSpec as P

BLOCK = 128
SLOTS = 16
LANES = 128
HALF = 64
MESH = pl.DeviceIdType.MESH

mixing = 0.75
lowest_logit = -1e30


def lane_pick(values, index):
    return jnp.take_along_axis(values, index, axis=1, mode="promise_in_bounds")


def kernel(
    n_row, n_col, neighbours, width,
    pattern_ref, query_ref, emb_ref, lab_ref, pos_ref, sharp_ref, out_ref,
    emb_all, lab_all, spread_all, code, part, rs_buf, w_all, dense,
    local_sem, emb_send, emb_recv, lab_send, lab_recv, spread_send, spread_recv,
    rs_send, rs_recv, w_send, w_recv,
):
    me_row = lax.axis_index("row")
    me_col = lax.axis_index("col")
    blocks = lab_ref.shape[0]
    pairs = blocks // 2
    packed = pos_ref.shape[0]
    chunk = packed // n_row
    classes = lab_ref.shape[2]

    def row_peer(d):
        return lax.rem(me_row + d, n_row)

    def col_peer(d):
        return lax.rem(me_col + d, n_col)

    barrier = pltpu.get_barrier_semaphore()
    for d in range(1, n_col):
        pl.semaphore_signal(barrier, inc=1, device_id=(me_row, col_peer(d)), device_id_type=MESH)
    for d in range(1, n_row):
        pl.semaphore_signal(barrier, inc=1, device_id=(row_peer(d), me_col), device_id_type=MESH)
    pl.semaphore_wait(barrier, n_col + n_row - 2)

    mine = pl.ds(me_col * blocks, blocks)

    def gather_copies(src, whole, send, recv):
        return [
            pltpu.make_async_remote_copy(
                src_ref=src,
                dst_ref=whole.at[mine],
                send_sem=send.at[d],
                recv_sem=recv.at[d],
                device_id=(me_row, col_peer(d)),
                device_id_type=MESH,
            )
            for d in range(1, n_col)
        ]

    emb_copies = gather_copies(emb_ref, emb_all, emb_send, emb_recv)
    lab_copies = gather_copies(lab_ref, lab_all, lab_send, lab_recv)
    for copy in emb_copies:
        copy.start()
    own_emb = pltpu.make_async_copy(emb_ref, emb_all.at[mine], local_sem.at[0])
    own_emb.start()
    for copy in lab_copies:
        copy.start()
    own_lab = pltpu.make_async_copy(lab_ref, lab_all.at[mine], local_sem.at[1])
    own_lab.start()

    lane8 = lax.broadcasted_iota(jnp.int32, (8, LANES), 1)

    def encode(g, _):
        rows = pl.ds(pl.multiple_of(g * 8, 8), 8)
        pos = pos_ref[rows, :]
        inside = pos & (BLOCK - 1)
        slot = pos >> 7
        number = (lane8 & (HALF - 1)) << ((slot & 3) * 8)
        words = [jnp.where((slot >> 2) == q, number, 0) for q in range(4)]
        for h in range(2):
            acc = [jnp.full((8, LANES), 0x40404040 * h, jnp.int32) for _ in range(4)]
            for n in range(1, neighbours + 1):
                at = h * HALF + n
                hit = jnp.broadcast_to(inside[:, at : at + 1], (8, LANES)) == lane8
                for q in range(4):
                    word = jnp.broadcast_to(words[q][:, at : at + 1], (8, LANES))
                    acc[q] = acc[q] | jnp.where(hit, word, 0)
            for q in range(4):
                code[h * 4 + q, rows, :] = acc[q]
        return 0

    lax.fori_loop(0, packed // 8, encode, 0)

    own_emb.wait()
    for copy in emb_copies:
        copy.wait()

    lower = lax.broadcasted_iota(jnp.int32, (BLOCK, LANES), 1) < HALF

    def score(b, _):
        rows = pl.ds(pl.multiple_of(b * BLOCK, BLOCK), BLOCK)
        pos = pos_ref[rows, :]
        inside = pos & (BLOCK - 1)
        slot = pos >> 7
        acc = jnp.zeros((BLOCK, LANES), jnp.float32)
        for k in range(0, SLOTS, 2):
            picked = [None, None]
            for h in range(2):
                block = b + h * pairs
                q_rows = pl.ds(pl.multiple_of(block * BLOCK, BLOCK), BLOCK)
                cand = jnp.concatenate(
                    [emb_all[pattern_ref[block, k]], emb_all[pattern_ref[block, k + 1]]], axis=1
                )
                picked[h] = jnp.dot(query_ref[q_rows, :], cand, preferred_element_type=jnp.float32)
            for u in range(2):
                cols = slice(u * LANES, (u + 1) * LANES)
                got = jnp.where(
                    lower, lane_pick(picked[0][:, cols], inside), lane_pick(picked[1][:, cols], inside)
                )
                acc = jnp.where(slot == k + u, got, acc)
        part[rows, :] = acc
        return 0

    lax.fori_loop(0, pairs, score, 0)

    rs_copies = [
        pltpu.make_async_remote_copy(
            src_ref=part.at[pl.ds(row_peer(d) * chunk, chunk)],
            dst_ref=rs_buf.at[d],
            send_sem=rs_send.at[d],
            recv_sem=rs_recv.at[d],
            device_id=(row_peer(d), me_col),
            device_id_type=MESH,
        )
        for d in range(1, n_row)
    ]
    for copy in rs_copies:
        copy.start()
    my_rows = pl.ds(pl.multiple_of(me_row * chunk, chunk), chunk)
    total = part[my_rows, :]
    for d, copy in enumerate(rs_copies):
        copy.wait()
        total = total + rs_buf[d + 1]

    low = lax.broadcasted_iota(jnp.int32, (chunk, LANES), 1) < HALF
    valid = pos_ref[my_rows, :] >= 0
    logits = jnp.where(valid, total / math.sqrt(width) * sharp_ref[my_rows, :], lowest_logit)

    def by_half(reduce, values, neutral):
        first = reduce(jnp.where(low, values, neutral), axis=1, keepdims=True)
        second = reduce(jnp.where(low, neutral, values), axis=1, keepdims=True)
        return jnp.where(low, first, second)

    top = by_half(jnp.max, logits, lowest_logit)
    expo = jnp.where(valid, jnp.exp(logits - top), 0.0)
    sums = by_half(jnp.sum, expo, 0.0)
    w_all[my_rows, :] = (expo / sums).astype(jnp.bfloat16)

    w_copies = [
        pltpu.make_async_remote_copy(
            src_ref=w_all.at[my_rows],
            dst_ref=w_all.at[my_rows],
            send_sem=w_send.at[d],
            recv_sem=w_recv.at[d],
            device_id=(row_peer(d), me_col),
            device_id_type=MESH,
        )
        for d in range(1, n_row)
    ]
    for copy in w_copies:
        copy.start()
    for copy in w_copies:
        copy.wait()
    own_lab.wait()
    for copy in lab_copies:
        copy.wait()

    def blend(acc, block):
        return (mixing * acc + (1.0 - mixing) * lab_ref[block].astype(jnp.float32)).astype(
            jnp.bfloat16
        )

    def first_round(b, _):
        rows = pl.ds(pl.multiple_of(b * BLOCK, BLOCK), BLOCK)
        weights = w_all[rows, :].astype(jnp.float32)
        for h in range(2):
            block = b + h * pairs
            acc = jnp.zeros((BLOCK, classes), jnp.float32)
            for k in range(0, SLOTS, 2):
                pieces = []
                for u in range(k, k + 2):
                    index = (code[h * 4 + u // 4, rows, :] >> (8 * (u % 4))) & 0x7F
                    pieces.append(lane_pick(weights, index).astype(jnp.bfloat16))
                wide = jnp.concatenate(pieces, axis=1)
                dense[block, :, k * BLOCK : (k + 2) * BLOCK] = wide
                cand = jnp.concatenate(
                    [lab_all[pattern_ref[block, k]], lab_all[pattern_ref[block, k + 1]]], axis=0
                )
                acc += jnp.dot(wide, cand, preferred_element_type=jnp.float32)
            spread_all[me_col * blocks + block] = blend(acc, block)
        return 0

    lax.fori_loop(0, pairs, first_round, 0)

    spread_copies = gather_copies(spread_all.at[mine], spread_all, spread_send, spread_recv)
    for copy in spread_copies:
        copy.start()
    for copy in spread_copies:
        copy.wait()

    def second_round(block, _):
        acc = jnp.zeros((BLOCK, classes), jnp.float32)
        for k in range(0, SLOTS, 2):
            cand = jnp.concatenate(
                [spread_all[pattern_ref[block, k]], spread_all[pattern_ref[block, k + 1]]], axis=0
            )
            acc += jnp.dot(
                dense[block, :, k * BLOCK : (k + 2) * BLOCK], cand, preferred_element_type=jnp.float32
            )
        out_ref[block] = blend(acc, block)
        return 0

    lax.fori_loop(0, blocks, second_round, 0)


def body(embeds, labels, sharpness, pattern, mask_pos):
    rows_here, width = embeds.shape
    classes = labels.shape[1]
    neighbours = mask_pos.shape[1]
    n_col = lax.axis_size("col")
    n_row = lax.axis_size("row")
    row_pos = lax.axis_index("row")
    blocks = rows_here // BLOCK
    packed = rows_here // 2
    features = width // n_row
    per_device = classes // n_row
    wide = -(-per_device // LANES) * LANES

    query = lax.dynamic_slice_in_dim(embeds, row_pos * features, features, 1)
    emb = query.reshape(blocks, BLOCK, features).transpose(0, 2, 1)
    lab = lax.dynamic_slice_in_dim(labels, row_pos * per_device, per_device, 1)
    lab = jnp.pad(lab, ((0, 0), (0, wide - per_device))).reshape(blocks, BLOCK, wide)
    pos = jnp.pad(mask_pos, ((0, 0), (1, HALF - 1 - neighbours)), constant_values=-1)
    pos = jnp.concatenate([pos[:packed], pos[packed:]], axis=1)
    sharp = jnp.concatenate(
        [
            jnp.broadcast_to(sharpness[:packed, None], (packed, HALF)),
            jnp.broadcast_to(sharpness[packed:, None], (packed, HALF)),
        ],
        axis=1,
    )
    total_blocks = n_col * blocks
    vmem = pl.BlockSpec(memory_space=pltpu.VMEM)
    out = pl.pallas_call(
        functools.partial(kernel, n_row, n_col, neighbours, width),
        out_shape=jax.ShapeDtypeStruct((blocks, BLOCK, wide), jnp.bfloat16),
        in_specs=[pl.BlockSpec(memory_space=pltpu.SMEM)] + [vmem] * 5,
        out_specs=vmem,
        scratch_shapes=[
            pltpu.VMEM((total_blocks, features, BLOCK), jnp.bfloat16),
            pltpu.VMEM((total_blocks, BLOCK, wide), jnp.bfloat16),
            pltpu.VMEM((total_blocks, BLOCK, wide), jnp.bfloat16),
            pltpu.VMEM((8, packed, LANES), jnp.int32),
            pltpu.VMEM((packed, LANES), jnp.float32),
            pltpu.VMEM((n_row, packed // n_row, LANES), jnp.float32),
            pltpu.VMEM((packed, LANES), jnp.bfloat16),
            pltpu.VMEM((blocks, BLOCK, SLOTS * BLOCK), jnp.bfloat16),
            pltpu.SemaphoreType.DMA((2,)),
        ]
        + [pltpu.SemaphoreType.DMA((n_col,))] * 6
        + [pltpu.SemaphoreType.DMA((n_row,))] * 4,
        compiler_params=pltpu.CompilerParams(
            collective_id=0, has_side_effects=True, vmem_limit_bytes=48 * 1024 * 1024
        ),
    )(pattern, query, emb, lab, pos, sharp)
    return out.reshape(rows_here, wide)[:, :per_device]


def solution(mesh):
    placed = (P("col", None), P("col", None), P("col"), P("col", None), P("col", None))
    return jax.shard_map(
        body, mesh=mesh, in_specs=placed, out_specs=P("col", "row"), check_vma=False
    )
```

```python
import functools
import math

import jax
import jax.numpy as jnp
from jax import lax
from jax.experimental import pallas as pl
from jax.experimental.pallas import tpu as pltpu
from jax.sharding import PartitionSpec as P

BLOCK = 128
SLOTS = 16
LANES = 128
HALF = 64
MESH = pl.DeviceIdType.MESH

mixing = 0.75
lowest_logit = -1e30


def lane_pick(values, index):
    return jnp.take_along_axis(values, index, axis=1, mode="promise_in_bounds")


class DirectGather:
    def __init__(self, own, whole, send, recv, local, n_col):
        row, me = lax.axis_index("row"), lax.axis_index("col")
        blocks = whole.shape[0] // n_col
        mine = pl.ds(me * blocks, blocks)
        self.local = None if own is None else pltpu.make_async_copy(own, whole.at[mine], local)
        self.copies = [
            pltpu.make_async_remote_copy(
                src_ref=whole.at[mine] if own is None else own,
                dst_ref=whole.at[mine],
                send_sem=send.at[d],
                recv_sem=recv.at[d],
                device_id=(row, lax.rem(me + d, n_col)),
                device_id_type=MESH,
            )
            for d in range(1, n_col)
        ]

    def start(self):
        for copy in self.copies:
            copy.start()
        if self.local is not None:
            self.local.start()

    def start_half(self, half):
        if half == 1:
            self.start()

    def forward_first(self):
        pass

    def forward_rest(self):
        pass

    def finish(self):
        if self.local is not None:
            self.local.wait()
        for copy in self.copies:
            copy.wait()


class PairwiseGather:
    def __init__(self, own, whole, send, recv, local, n_col):
        row, me = lax.axis_index("row"), lax.axis_index("col")
        blocks = whole.shape[0] // n_col
        part = blocks // 2
        core, x, y = me % 2, (me // 2) % 2, me // 4
        sib = me + 1 - 2 * core
        xn = me + 2 - 4 * x
        yn = me + 4 - 8 * y
        diagonal = xn + yn - me
        plan = [
            (me, 0, xn), (me, 1, yn), (me, 1, xn), (me, 0, yn), (me, 0, sib), (me, 1, sib),
            (xn, 0, yn), (yn, 1, xn), (xn, 0, sib), (yn, 1, sib), (xn, 1, sib), (yn, 0, sib),
            (diagonal, 0, sib), (diagonal, 1, sib),
        ]
        self.local = None
        if own is not None:
            self.local = pltpu.make_async_copy(own, whole.at[pl.ds(me * blocks, blocks)], local)
        self.copies = []
        for i, (owner, half, target) in enumerate(plan):
            there = whole.at[pl.ds(owner * blocks + half * part, part)]
            src = there if own is None or i >= 6 else own.at[pl.ds(half * part, part)]
            self.copies.append(
                pltpu.make_async_remote_copy(
                    src_ref=src,
                    dst_ref=there,
                    send_sem=send.at[i],
                    recv_sem=recv.at[i],
                    device_id=(row, target),
                    device_id_type=MESH,
                )
            )

    def start(self):
        for i in range(6):
            self.copies[i].start()
        if self.local is not None:
            self.local.start()

    def start_half(self, half):
        for i in ((0, 3, 4), (1, 2, 5))[half]:
            self.copies[i].start()

    def pass_on(self, arrived, onward):
        self.copies[arrived].wait_recv()
        for i in onward:
            self.copies[i].start()

    def forward_first(self):
        self.pass_on(0, (6, 8))
        self.pass_on(1, (7, 9))

    def forward_rest(self):
        self.pass_on(2, (10,))
        self.pass_on(3, (11,))
        self.pass_on(6, (12,))
        self.pass_on(7, (13,))

    def finish(self):
        if self.local is not None:
            self.local.wait()
        for i in (4, 5, 8, 9, 10, 11, 12, 13):
            self.copies[i].wait_recv()
        for copy in self.copies:
            copy.wait_send()


def kernel(
    n_row, n_col, neighbours, width,
    pattern_ref, query_ref, emb_ref, lab_ref, pos_ref, post_ref, sharp_ref, out_ref,
    emb_all, lab_all, spread_all, code, turned, number, part, rs_buf, w_all, dense,
    local_sem, emb_send, emb_recv, lab_send, lab_recv, spread_send, spread_recv,
    rs_send, rs_recv, w_send, w_recv,
):
    me_row = lax.axis_index("row")
    me_col = lax.axis_index("col")
    blocks = lab_ref.shape[0]
    pairs = blocks // 2
    packed = pos_ref.shape[0]
    chunk = packed // n_row
    classes = lab_ref.shape[2]

    def row_peer(d):
        return lax.rem(me_row + d, n_row)

    def col_peer(d):
        return lax.rem(me_col + d, n_col)

    barrier = pltpu.get_barrier_semaphore()
    for d in range(1, n_col):
        pl.semaphore_signal(barrier, inc=1, device_id=(me_row, col_peer(d)), device_id_type=MESH)
    for d in range(1, n_row):
        pl.semaphore_signal(barrier, inc=1, device_id=(row_peer(d), me_col), device_id_type=MESH)
    pl.semaphore_wait(barrier, n_col + n_row - 2)

    gather = PairwiseGather if n_col == 8 else DirectGather
    emb_gather = gather(emb_ref, emb_all, emb_send, emb_recv, local_sem.at[0], n_col)
    lab_gather = gather(lab_ref, lab_all, lab_send, lab_recv, local_sem.at[1], n_col)
    spread_gather = gather(None, spread_all, spread_send, spread_recv, None, n_col)

    tile = 32
    emb_gather.start()

    def encode(block, _):
        cols = pl.ds(pl.multiple_of(block * BLOCK, BLOCK), BLOCK)
        pos = post_ref[:, cols]
        slot = pos >> 7
        value = lax.broadcasted_iota(jnp.int32, (HALF, BLOCK), 0) << ((slot & 3) * 8)
        number[4] = pos & (BLOCK - 1)
        for q in range(4):
            number[q] = jnp.where((slot >> 2) == q, value, 0)
        side = block // pairs
        for at in range(0, BLOCK, tile):
            here = at + lax.broadcasted_iota(jnp.int32, (tile, BLOCK), 0)
            acc = [jnp.full((tile, BLOCK), 0x40404040 * side, jnp.int32) for _ in range(4)]
            for n in range(1, neighbours + 1):
                hit = jnp.broadcast_to(number[4, n : n + 1, :], (tile, BLOCK)) == here
                for q in range(4):
                    word = jnp.broadcast_to(number[q, n : n + 1, :], (tile, BLOCK))
                    acc[q] = acc[q] | jnp.where(hit, word, 0)
            for q in range(4):
                turned[q, at : at + tile, :] = acc[q]
        rows = pl.ds(pl.multiple_of((block - side * pairs) * BLOCK, BLOCK), BLOCK)
        for q in range(4):
            code[side * 4 + q, rows, :] = turned[q].T
        return 0

    lax.fori_loop(0, pairs, encode, 0)
    emb_gather.forward_first()
    lax.fori_loop(pairs, blocks, encode, 0)
    emb_gather.forward_rest()
    lab_gather.start()
    emb_gather.finish()

    lower = lax.broadcasted_iota(jnp.int32, (BLOCK, LANES), 1) < HALF

    def score(b, _):
        rows = pl.ds(pl.multiple_of(b * BLOCK, BLOCK), BLOCK)
        pos = pos_ref[rows, :]
        inside = pos & (BLOCK - 1)
        slot = pos >> 7
        acc = jnp.zeros((BLOCK, LANES), jnp.float32)
        for k in range(0, SLOTS, 2):
            picked = [None, None]
            for h in range(2):
                block = b + h * pairs
                q_rows = pl.ds(pl.multiple_of(block * BLOCK, BLOCK), BLOCK)
                cand = jnp.concatenate(
                    [emb_all[pattern_ref[block, k]], emb_all[pattern_ref[block, k + 1]]], axis=1
                )
                picked[h] = jnp.dot(query_ref[q_rows, :], cand, preferred_element_type=jnp.float32)
            for u in range(2):
                cols = slice(u * LANES, (u + 1) * LANES)
                got = jnp.where(
                    lower, lane_pick(picked[0][:, cols], inside), lane_pick(picked[1][:, cols], inside)
                )
                acc = jnp.where(slot == k + u, got, acc)
        part[rows, :] = acc
        return 0

    lax.fori_loop(0, pairs, score, 0)

    rs_copies = [
        pltpu.make_async_remote_copy(
            src_ref=part.at[pl.ds(row_peer(d) * chunk, chunk)],
            dst_ref=rs_buf.at[d],
            send_sem=rs_send.at[d],
            recv_sem=rs_recv.at[d],
            device_id=(row_peer(d), me_col),
            device_id_type=MESH,
        )
        for d in range(1, n_row)
    ]
    for copy in rs_copies:
        copy.start()
    lab_gather.forward_first()
    my_rows = pl.ds(pl.multiple_of(me_row * chunk, chunk), chunk)
    total = part[my_rows, :]
    for d, copy in enumerate(rs_copies):
        copy.wait()
        total = total + rs_buf[d + 1]

    low = lax.broadcasted_iota(jnp.int32, (chunk, LANES), 1) < HALF
    valid = pos_ref[my_rows, :] >= 0
    logits = jnp.where(valid, total / math.sqrt(width) * sharp_ref[my_rows, :], lowest_logit)

    def by_half(reduce, values, neutral):
        first = reduce(jnp.where(low, values, neutral), axis=1, keepdims=True)
        second = reduce(jnp.where(low, neutral, values), axis=1, keepdims=True)
        return jnp.where(low, first, second)

    top = by_half(jnp.max, logits, lowest_logit)
    expo = jnp.where(valid, jnp.exp(logits - top), 0.0)
    sums = by_half(jnp.sum, expo, 0.0)
    w_all[my_rows, :] = (expo / sums).astype(jnp.bfloat16)

    w_copies = [
        pltpu.make_async_remote_copy(
            src_ref=w_all.at[my_rows],
            dst_ref=w_all.at[my_rows],
            send_sem=w_send.at[d],
            recv_sem=w_recv.at[d],
            device_id=(row_peer(d), me_col),
            device_id_type=MESH,
        )
        for d in range(1, n_row)
    ]
    for copy in w_copies:
        copy.start()
    lab_gather.forward_rest()
    for copy in w_copies:
        copy.wait()
    lab_gather.finish()

    def blend(acc, block):
        return (mixing * acc + (1.0 - mixing) * lab_ref[block].astype(jnp.float32)).astype(
            jnp.bfloat16
        )

    def first_round(h, b, _):
        rows = pl.ds(pl.multiple_of(b * BLOCK, BLOCK), BLOCK)
        weights = w_all[rows, :].astype(jnp.float32)
        block = b + h * pairs
        acc = jnp.zeros((BLOCK, classes), jnp.float32)
        for k in range(0, SLOTS, 2):
            pieces = []
            for u in range(k, k + 2):
                index = (code[h * 4 + u // 4, rows, :] >> (8 * (u % 4))) & 0x7F
                pieces.append(lane_pick(weights, index).astype(jnp.bfloat16))
            wide = jnp.concatenate(pieces, axis=1)
            dense[block, :, k * BLOCK : (k + 2) * BLOCK] = wide
            cand = jnp.concatenate(
                [lab_all[pattern_ref[block, k]], lab_all[pattern_ref[block, k + 1]]], axis=0
            )
            acc += jnp.dot(wide, cand, preferred_element_type=jnp.float32)
        spread_all[me_col * blocks + block] = blend(acc, block)
        return 0

    for h in range(2):
        lax.fori_loop(0, pairs, functools.partial(first_round, h), 0)
        spread_gather.start_half(h)
    spread_gather.forward_first()
    spread_gather.forward_rest()
    spread_gather.finish()

    def second_round(block, _):
        acc = jnp.zeros((BLOCK, classes), jnp.float32)
        for k in range(0, SLOTS, 2):
            cand = jnp.concatenate(
                [spread_all[pattern_ref[block, k]], spread_all[pattern_ref[block, k + 1]]], axis=0
            )
            acc += jnp.dot(
                dense[block, :, k * BLOCK : (k + 2) * BLOCK], cand, preferred_element_type=jnp.float32
            )
        out_ref[block] = blend(acc, block)
        return 0

    lax.fori_loop(0, blocks, second_round, 0)


def body(embeds, labels, sharpness, pattern, mask_pos):
    rows_here, width = embeds.shape
    classes = labels.shape[1]
    neighbours = mask_pos.shape[1]
    n_col = lax.axis_size("col")
    n_row = lax.axis_size("row")
    row_pos = lax.axis_index("row")
    blocks = rows_here // BLOCK
    packed = rows_here // 2
    features = width // n_row
    per_device = classes // n_row
    wide = -(-per_device // LANES) * LANES

    query = lax.dynamic_slice_in_dim(embeds, row_pos * features, features, 1)
    emb = query.reshape(blocks, BLOCK, features).transpose(0, 2, 1)
    lab = lax.dynamic_slice_in_dim(labels, row_pos * per_device, per_device, 1)
    lab = jnp.pad(lab, ((0, 0), (0, wide - per_device))).reshape(blocks, BLOCK, wide)
    pos = jnp.pad(mask_pos, ((0, 0), (1, HALF - 1 - neighbours)), constant_values=-1)
    post = pos.T
    pos = jnp.concatenate([pos[:packed], pos[packed:]], axis=1)
    sharp = jnp.concatenate(
        [
            jnp.broadcast_to(sharpness[:packed, None], (packed, HALF)),
            jnp.broadcast_to(sharpness[packed:, None], (packed, HALF)),
        ],
        axis=1,
    )
    total_blocks = n_col * blocks
    vmem = pl.BlockSpec(memory_space=pltpu.VMEM)
    out = pl.pallas_call(
        functools.partial(kernel, n_row, n_col, neighbours, width),
        out_shape=jax.ShapeDtypeStruct((blocks, BLOCK, wide), jnp.bfloat16),
        in_specs=[pl.BlockSpec(memory_space=pltpu.SMEM)] + [vmem] * 6,
        out_specs=vmem,
        scratch_shapes=[
            pltpu.VMEM((total_blocks, features, BLOCK), jnp.bfloat16),
            pltpu.VMEM((total_blocks, BLOCK, wide), jnp.bfloat16),
            pltpu.VMEM((total_blocks, BLOCK, wide), jnp.bfloat16),
            pltpu.VMEM((8, packed, LANES), jnp.int32),
            pltpu.VMEM((4, BLOCK, BLOCK), jnp.int32),
            pltpu.VMEM((5, HALF, BLOCK), jnp.int32),
            pltpu.VMEM((packed, LANES), jnp.float32),
            pltpu.VMEM((n_row, packed // n_row, LANES), jnp.float32),
            pltpu.VMEM((packed, LANES), jnp.bfloat16),
            pltpu.VMEM((blocks, BLOCK, SLOTS * BLOCK), jnp.bfloat16),
            pltpu.SemaphoreType.DMA((2,)),
        ]
        + [pltpu.SemaphoreType.DMA((max(n_col, 14),))] * 6
        + [pltpu.SemaphoreType.DMA((n_row,))] * 4,
        compiler_params=pltpu.CompilerParams(
            collective_id=0, has_side_effects=True, vmem_limit_bytes=48 * 1024 * 1024
        ),
    )(pattern, query, emb, lab, pos, post, sharp)
    return out.reshape(rows_here, wide)[:, :per_device]


def solution(mesh):
    placed = (P("col", None), P("col", None), P("col"), P("col", None), P("col", None))
    return jax.shard_map(
        body, mesh=mesh, in_specs=placed, out_specs=P("col", "row"), check_vma=False
    )
```

```python
import functools
import math

import jax
import jax.numpy as jnp
from jax import lax
from jax.experimental import pallas as pl
from jax.experimental.pallas import tpu as pltpu
from jax.sharding import PartitionSpec as P

BLOCK = 128
SLOTS = 16
LANES = 128
HALF = 64
MESH = pl.DeviceIdType.MESH

mixing = 0.75
lowest_logit = -1e30


def lane_pick(values, index):
    return jnp.take_along_axis(values, index, axis=1, mode="promise_in_bounds")


class DirectGather:
    def __init__(self, own, whole, send, recv, local, n_col):
        row, me = lax.axis_index("row"), lax.axis_index("col")
        blocks = whole.shape[0] // n_col
        mine = pl.ds(me * blocks, blocks)
        self.local = None if own is None else pltpu.make_async_copy(own, whole.at[mine], local)
        self.copies = [
            pltpu.make_async_remote_copy(
                src_ref=whole.at[mine] if own is None else own,
                dst_ref=whole.at[mine],
                send_sem=send.at[d],
                recv_sem=recv.at[d],
                device_id=(row, lax.rem(me + d, n_col)),
                device_id_type=MESH,
            )
            for d in range(1, n_col)
        ]

    def start(self):
        for copy in self.copies:
            copy.start()
        if self.local is not None:
            self.local.start()

    def start_half(self, half):
        if half == 1:
            self.start()

    def forward_first(self):
        pass

    def forward_rest(self):
        pass

    def finish(self):
        if self.local is not None:
            self.local.wait()
        for copy in self.copies:
            copy.wait()


class PairwiseGather:
    def __init__(self, own, whole, send, recv, local, n_col):
        row, me = lax.axis_index("row"), lax.axis_index("col")
        blocks = whole.shape[0] // n_col
        part = blocks // 2
        core, x, y = me % 2, (me // 2) % 2, me // 4
        sib = me + 1 - 2 * core
        xn = me + 2 - 4 * x
        yn = me + 4 - 8 * y
        diagonal = xn + yn - me
        plan = [
            (me, 0, xn), (me, 1, yn), (me, 1, xn), (me, 0, yn), (me, 0, sib), (me, 1, sib),
            (xn, 0, yn), (yn, 1, xn), (xn, 0, sib), (yn, 1, sib), (xn, 1, sib), (yn, 0, sib),
            (diagonal, 0, sib), (diagonal, 1, sib),
        ]
        self.local = None
        if own is not None:
            self.local = pltpu.make_async_copy(own, whole.at[pl.ds(me * blocks, blocks)], local)
        self.copies = []
        for i, (owner, half, target) in enumerate(plan):
            there = whole.at[pl.ds(owner * blocks + half * part, part)]
            src = there if own is None or i >= 6 else own.at[pl.ds(half * part, part)]
            self.copies.append(
                pltpu.make_async_remote_copy(
                    src_ref=src,
                    dst_ref=there,
                    send_sem=send.at[i],
                    recv_sem=recv.at[i],
                    device_id=(row, target),
                    device_id_type=MESH,
                )
            )

    def start(self):
        for i in range(6):
            self.copies[i].start()
        if self.local is not None:
            self.local.start()

    def start_half(self, half):
        for i in ((0, 3, 4), (1, 2, 5))[half]:
            self.copies[i].start()

    def pass_on(self, arrived, onward):
        self.copies[arrived].wait_recv()
        for i in onward:
            self.copies[i].start()

    def forward_first(self):
        self.pass_on(0, (6, 8))
        self.pass_on(1, (7, 9))

    def forward_rest(self):
        self.pass_on(2, (10,))
        self.pass_on(3, (11,))
        self.pass_on(6, (12,))
        self.pass_on(7, (13,))

    def finish(self):
        if self.local is not None:
            self.local.wait()
        for i in (4, 5, 8, 9, 10, 11, 12, 13):
            self.copies[i].wait_recv()
        for copy in self.copies:
            copy.wait_send()


def kernel(
    n_row, n_col, neighbours, width,
    pattern_ref, query_ref, emb_ref, lab_ref, post_ref, sharpt_ref, out_ref,
    pos_ref, sharp_ref, emb_all, lab_all, spread_all, code, turned, number, part, rs_buf, w_all, dense,
    local_sem, emb_send, emb_recv, lab_send, lab_recv, spread_send, spread_recv,
    rs_send, rs_recv, w_send, w_recv,
):
    me_row = lax.axis_index("row")
    me_col = lax.axis_index("col")
    blocks = lab_ref.shape[0]
    pairs = blocks // 2
    packed = pos_ref.shape[0]
    chunk = packed // n_row
    classes = lab_ref.shape[2]

    def row_peer(d):
        return lax.rem(me_row + d, n_row)

    def col_peer(d):
        return lax.rem(me_col + d, n_col)

    barrier = pltpu.get_barrier_semaphore()
    for d in range(1, n_col):
        pl.semaphore_signal(barrier, inc=1, device_id=(me_row, col_peer(d)), device_id_type=MESH)
    for d in range(1, n_row):
        pl.semaphore_signal(barrier, inc=1, device_id=(row_peer(d), me_col), device_id_type=MESH)
    pl.semaphore_wait(barrier, n_col + n_row - 2)

    gather = PairwiseGather if n_col == 8 else DirectGather
    emb_gather = gather(emb_ref, emb_all, emb_send, emb_recv, local_sem.at[0], n_col)
    lab_gather = gather(lab_ref, lab_all, lab_send, lab_recv, local_sem.at[1], n_col)
    spread_gather = gather(None, spread_all, spread_send, spread_recv, None, n_col)

    tile = 32
    emb_gather.start()

    for b in range(pairs):
        rows = slice(b * BLOCK, (b + 1) * BLOCK)
        others = slice((b + pairs) * BLOCK, (b + pairs + 1) * BLOCK)
        pos_ref[rows, :] = jnp.concatenate([post_ref[:, rows], post_ref[:, others]], axis=0).T
        sharp_ref[rows, :] = jnp.concatenate(
            [
                jnp.broadcast_to(sharpt_ref[:, rows], (HALF, BLOCK)),
                jnp.broadcast_to(sharpt_ref[:, others], (HALF, BLOCK)),
            ],
            axis=0,
        ).T

    def encode(block, _):
        cols = pl.ds(pl.multiple_of(block * BLOCK, BLOCK), BLOCK)
        pos = post_ref[:, cols]
        slot = pos >> 7
        value = lax.broadcasted_iota(jnp.int32, (HALF, BLOCK), 0) << ((slot & 3) * 8)
        number[4] = pos & (BLOCK - 1)
        for q in range(4):
            number[q] = jnp.where((slot >> 2) == q, value, 0)
        side = block // pairs
        for at in range(0, BLOCK, tile):
            here = at + lax.broadcasted_iota(jnp.int32, (tile, BLOCK), 0)
            acc = [jnp.full((tile, BLOCK), 0x40404040 * side, jnp.int32) for _ in range(4)]
            for n in range(1, neighbours + 1):
                hit = jnp.broadcast_to(number[4, n : n + 1, :], (tile, BLOCK)) == here
                for q in range(4):
                    word = jnp.broadcast_to(number[q, n : n + 1, :], (tile, BLOCK))
                    acc[q] = acc[q] | jnp.where(hit, word, 0)
            for q in range(4):
                turned[q, at : at + tile, :] = acc[q]
        rows = pl.ds(pl.multiple_of((block - side * pairs) * BLOCK, BLOCK), BLOCK)
        for q in range(4):
            code[side * 4 + q, rows, :] = turned[q].T
        return 0

    lax.fori_loop(0, pairs, encode, 0)
    emb_gather.forward_first()
    lax.fori_loop(pairs, blocks, encode, 0)
    emb_gather.forward_rest()
    lab_gather.start()
    emb_gather.finish()

    lower = lax.broadcasted_iota(jnp.int32, (BLOCK, LANES), 1) < HALF

    def score(b, _):
        rows = pl.ds(pl.multiple_of(b * BLOCK, BLOCK), BLOCK)
        pos = pos_ref[rows, :]
        inside = pos & (BLOCK - 1)
        slot = pos >> 7
        acc = jnp.zeros((BLOCK, LANES), jnp.float32)
        for k in range(0, SLOTS, 2):
            picked = [None, None]
            for h in range(2):
                block = b + h * pairs
                q_rows = pl.ds(pl.multiple_of(block * BLOCK, BLOCK), BLOCK)
                cand = jnp.concatenate(
                    [emb_all[pattern_ref[block, k]], emb_all[pattern_ref[block, k + 1]]], axis=1
                )
                picked[h] = jnp.dot(query_ref[q_rows, :], cand, preferred_element_type=jnp.float32)
            for u in range(2):
                cols = slice(u * LANES, (u + 1) * LANES)
                got = jnp.where(
                    lower, lane_pick(picked[0][:, cols], inside), lane_pick(picked[1][:, cols], inside)
                )
                acc = jnp.where(slot == k + u, got, acc)
        part[rows, :] = acc
        return 0

    lax.fori_loop(0, pairs, score, 0)

    rs_copies = [
        pltpu.make_async_remote_copy(
            src_ref=part.at[pl.ds(row_peer(d) * chunk, chunk)],
            dst_ref=rs_buf.at[d],
            send_sem=rs_send.at[d],
            recv_sem=rs_recv.at[d],
            device_id=(row_peer(d), me_col),
            device_id_type=MESH,
        )
        for d in range(1, n_row)
    ]
    for copy in rs_copies:
        copy.start()
    lab_gather.forward_first()
    my_rows = pl.ds(pl.multiple_of(me_row * chunk, chunk), chunk)
    total = part[my_rows, :]
    for d, copy in enumerate(rs_copies):
        copy.wait()
        total = total + rs_buf[d + 1]

    low = lax.broadcasted_iota(jnp.int32, (chunk, LANES), 1) < HALF
    valid = pos_ref[my_rows, :] >= 0
    logits = jnp.where(valid, total / math.sqrt(width) * sharp_ref[my_rows, :], lowest_logit)

    def by_half(reduce, values, neutral):
        first = reduce(jnp.where(low, values, neutral), axis=1, keepdims=True)
        second = reduce(jnp.where(low, neutral, values), axis=1, keepdims=True)
        return jnp.where(low, first, second)

    top = by_half(jnp.max, logits, lowest_logit)
    expo = jnp.where(valid, jnp.exp(logits - top), 0.0)
    sums = by_half(jnp.sum, expo, 0.0)
    w_all[my_rows, :] = (expo / sums).astype(jnp.bfloat16)

    w_copies = [
        pltpu.make_async_remote_copy(
            src_ref=w_all.at[my_rows],
            dst_ref=w_all.at[my_rows],
            send_sem=w_send.at[d],
            recv_sem=w_recv.at[d],
            device_id=(row_peer(d), me_col),
            device_id_type=MESH,
        )
        for d in range(1, n_row)
    ]
    for copy in w_copies:
        copy.start()
    lab_gather.forward_rest()
    for copy in w_copies:
        copy.wait()
    lab_gather.finish()

    def blend(acc, block):
        return (mixing * acc + (1.0 - mixing) * lab_ref[block].astype(jnp.float32)).astype(
            jnp.bfloat16
        )

    def first_round(h, b, _):
        rows = pl.ds(pl.multiple_of(b * BLOCK, BLOCK), BLOCK)
        weights = w_all[rows, :].astype(jnp.float32)
        block = b + h * pairs
        acc = jnp.zeros((BLOCK, classes), jnp.float32)
        for k in range(0, SLOTS, 2):
            pieces = []
            for u in range(k, k + 2):
                index = (code[h * 4 + u // 4, rows, :] >> (8 * (u % 4))) & 0x7F
                pieces.append(lane_pick(weights, index).astype(jnp.bfloat16))
            wide = jnp.concatenate(pieces, axis=1)
            dense[block, :, k * BLOCK : (k + 2) * BLOCK] = wide
            cand = jnp.concatenate(
                [lab_all[pattern_ref[block, k]], lab_all[pattern_ref[block, k + 1]]], axis=0
            )
            acc += jnp.dot(wide, cand, preferred_element_type=jnp.float32)
        spread_all[me_col * blocks + block] = blend(acc, block)
        return 0

    for h in range(2):
        lax.fori_loop(0, pairs, functools.partial(first_round, h), 0)
        spread_gather.start_half(h)
    spread_gather.forward_first()
    spread_gather.forward_rest()
    spread_gather.finish()

    def second_round(block, _):
        acc = jnp.zeros((BLOCK, classes), jnp.float32)
        for k in range(0, SLOTS, 2):
            cand = jnp.concatenate(
                [spread_all[pattern_ref[block, k]], spread_all[pattern_ref[block, k + 1]]], axis=0
            )
            acc += jnp.dot(
                dense[block, :, k * BLOCK : (k + 2) * BLOCK], cand, preferred_element_type=jnp.float32
            )
        out_ref[block] = blend(acc, block)
        return 0

    lax.fori_loop(0, blocks, second_round, 0)


def body(embeds, labels, sharpness, pattern, mask_pos):
    rows_here, width = embeds.shape
    classes = labels.shape[1]
    neighbours = mask_pos.shape[1]
    n_col = lax.axis_size("col")
    n_row = lax.axis_size("row")
    row_pos = lax.axis_index("row")
    blocks = rows_here // BLOCK
    packed = rows_here // 2
    features = width // n_row
    per_device = classes // n_row
    wide = -(-per_device // LANES) * LANES

    query = lax.dynamic_slice_in_dim(embeds, row_pos * features, features, 1)
    emb = query.reshape(blocks, BLOCK, features).transpose(0, 2, 1)
    lab = lax.dynamic_slice_in_dim(labels, row_pos * per_device, per_device, 1)
    lab = jnp.pad(lab, ((0, 0), (0, wide - per_device))).reshape(blocks, BLOCK, wide)
    pos = jnp.pad(mask_pos, ((0, 0), (1, HALF - 1 - neighbours)), constant_values=-1)
    post = pos.T
    sharpt = sharpness.reshape(1, rows_here)
    total_blocks = n_col * blocks
    vmem = pl.BlockSpec(memory_space=pltpu.VMEM)
    out = pl.pallas_call(
        functools.partial(kernel, n_row, n_col, neighbours, width),
        out_shape=jax.ShapeDtypeStruct((blocks, BLOCK, wide), jnp.bfloat16),
        in_specs=[pl.BlockSpec(memory_space=pltpu.SMEM)] + [vmem] * 5,
        out_specs=vmem,
        scratch_shapes=[
            pltpu.VMEM((packed, LANES), jnp.int32),
            pltpu.VMEM((packed, LANES), jnp.float32),
            pltpu.VMEM((total_blocks, features, BLOCK), jnp.bfloat16),
            pltpu.VMEM((total_blocks, BLOCK, wide), jnp.bfloat16),
            pltpu.VMEM((total_blocks, BLOCK, wide), jnp.bfloat16),
            pltpu.VMEM((8, packed, LANES), jnp.int32),
            pltpu.VMEM((4, BLOCK, BLOCK), jnp.int32),
            pltpu.VMEM((5, HALF, BLOCK), jnp.int32),
            pltpu.VMEM((packed, LANES), jnp.float32),
            pltpu.VMEM((n_row, packed // n_row, LANES), jnp.float32),
            pltpu.VMEM((packed, LANES), jnp.bfloat16),
            pltpu.VMEM((blocks, BLOCK, SLOTS * BLOCK), jnp.bfloat16),
            pltpu.SemaphoreType.DMA((2,)),
        ]
        + [pltpu.SemaphoreType.DMA((max(n_col, 14),))] * 6
        + [pltpu.SemaphoreType.DMA((n_row,))] * 4,
        compiler_params=pltpu.CompilerParams(
            collective_id=0, has_side_effects=True, vmem_limit_bytes=48 * 1024 * 1024
        ),
    )(pattern, query, emb, lab, post, sharpt)
    return out.reshape(rows_here, wide)[:, :per_device]


def solution(mesh):
    placed = (P("col", None), P("col", None), P("col"), P("col", None), P("col", None))
    return jax.shard_map(
        body, mesh=mesh, in_specs=placed, out_specs=P("col", "row"), check_vma=False
    )
```

```python
import functools
import math

import jax
import jax.numpy as jnp
from jax import lax
from jax.experimental import pallas as pl
from jax.experimental.pallas import tpu as pltpu
from jax.sharding import PartitionSpec as P

BLOCK = 128
SLOTS = 16
LANES = 128
HALF = 64
MESH = pl.DeviceIdType.MESH

mixing = 0.75
lowest_logit = -1e30


def lane_pick(values, index):
    return jnp.take_along_axis(values, index, axis=1, mode="promise_in_bounds")


class DirectGather:
    def __init__(self, own, whole, send, recv, local, n_col):
        row, me = lax.axis_index("row"), lax.axis_index("col")
        blocks = whole.shape[0] // n_col
        mine = pl.ds(me * blocks, blocks)
        self.local = None if own is None else pltpu.make_async_copy(own, whole.at[mine], local)
        self.copies = [
            pltpu.make_async_remote_copy(
                src_ref=whole.at[mine] if own is None else own,
                dst_ref=whole.at[mine],
                send_sem=send.at[d],
                recv_sem=recv.at[d],
                device_id=(row, lax.rem(me + d, n_col)),
                device_id_type=MESH,
            )
            for d in range(1, n_col)
        ]

    def start(self):
        for copy in self.copies:
            copy.start()
        if self.local is not None:
            self.local.start()

    def start_half(self, half):
        if half == 1:
            self.start()

    def forward_first(self):
        pass

    def forward_rest(self):
        pass

    def finish(self):
        if self.local is not None:
            self.local.wait()
        for copy in self.copies:
            copy.wait()


class PairwiseGather:
    def __init__(self, own, whole, send, recv, local, n_col):
        row, me = lax.axis_index("row"), lax.axis_index("col")
        blocks = whole.shape[0] // n_col
        part = blocks // 2
        core, x, y = me % 2, (me // 2) % 2, me // 4
        sib = me + 1 - 2 * core
        xn = me + 2 - 4 * x
        yn = me + 4 - 8 * y
        diagonal = xn + yn - me
        plan = [
            (me, 0, xn), (me, 1, yn), (me, 1, xn), (me, 0, yn), (me, 0, sib), (me, 1, sib),
            (xn, 0, yn), (yn, 1, xn), (xn, 0, sib), (yn, 1, sib), (xn, 1, sib), (yn, 0, sib),
            (diagonal, 0, sib), (diagonal, 1, sib),
        ]
        self.local = None
        if own is not None:
            self.local = pltpu.make_async_copy(own, whole.at[pl.ds(me * blocks, blocks)], local)
        self.copies = []
        for i, (owner, half, target) in enumerate(plan):
            there = whole.at[pl.ds(owner * blocks + half * part, part)]
            src = there if own is None or i >= 6 else own.at[pl.ds(half * part, part)]
            self.copies.append(
                pltpu.make_async_remote_copy(
                    src_ref=src,
                    dst_ref=there,
                    send_sem=send.at[i],
                    recv_sem=recv.at[i],
                    device_id=(row, target),
                    device_id_type=MESH,
                )
            )

    def start(self):
        for i in range(6):
            self.copies[i].start()
        if self.local is not None:
            self.local.start()

    def start_half(self, half):
        for i in ((0, 3, 4), (1, 2, 5))[half]:
            self.copies[i].start()

    def pass_on(self, arrived, onward):
        self.copies[arrived].wait_recv()
        for i in onward:
            self.copies[i].start()

    def forward_first(self):
        self.pass_on(0, (6, 8))
        self.pass_on(1, (7, 9))

    def forward_rest(self):
        self.pass_on(2, (10,))
        self.pass_on(3, (11,))
        self.pass_on(6, (12,))
        self.pass_on(7, (13,))

    def finish(self):
        if self.local is not None:
            self.local.wait()
        for i in (4, 5, 8, 9, 10, 11, 12, 13):
            self.copies[i].wait_recv()
        for copy in self.copies:
            copy.wait_send()


def kernel(
    n_row, n_col, neighbours, width,
    pattern_ref, query_ref, emb_ref, lab_ref, post_ref, sharpt_ref, out_ref,
    pos_ref, sharp_ref, emb_all, lab_all, spread_all, code, turned, number, part, rs_buf, w_all, dense,
    local_sem, emb_send, emb_recv, lab_send, lab_recv, spread_send, spread_recv,
    rs_send, rs_recv, w_send, w_recv,
):
    me_row = lax.axis_index("row")
    me_col = lax.axis_index("col")
    blocks = lab_ref.shape[0]
    pairs = blocks // 2
    packed = pos_ref.shape[0]
    chunk = packed // n_row
    classes = lab_ref.shape[2]

    def row_peer(d):
        return lax.rem(me_row + d, n_row)

    def col_peer(d):
        return lax.rem(me_col + d, n_col)

    barrier = pltpu.get_barrier_semaphore()
    for d in range(1, n_col):
        pl.semaphore_signal(barrier, inc=1, device_id=(me_row, col_peer(d)), device_id_type=MESH)
    for d in range(1, n_row):
        pl.semaphore_signal(barrier, inc=1, device_id=(row_peer(d), me_col), device_id_type=MESH)
    pl.semaphore_wait(barrier, n_col + n_row - 2)

    gather = PairwiseGather if n_col == 8 else DirectGather
    emb_gather = gather(emb_ref, emb_all, emb_send, emb_recv, local_sem.at[0], n_col)
    lab_gather = gather(lab_ref, lab_all, lab_send, lab_recv, local_sem.at[1], n_col)
    spread_gather = gather(None, spread_all, spread_send, spread_recv, None, n_col)

    tile = 32
    emb_gather.start()

    for b in range(pairs):
        rows = slice(b * BLOCK, (b + 1) * BLOCK)
        others = slice((b + pairs) * BLOCK, (b + pairs + 1) * BLOCK)
        pos_ref[rows, :] = jnp.concatenate([post_ref[:, rows], post_ref[:, others]], axis=0).T
        sharp_ref[rows, :] = jnp.concatenate(
            [
                jnp.broadcast_to(sharpt_ref[:, rows], (HALF, BLOCK)),
                jnp.broadcast_to(sharpt_ref[:, others], (HALF, BLOCK)),
            ],
            axis=0,
        ).T

    def encode(block, _):
        cols = pl.ds(pl.multiple_of(block * BLOCK, BLOCK), BLOCK)
        pos = post_ref[:, cols]
        slot = pos >> 7
        value = lax.broadcasted_iota(jnp.int32, (HALF, BLOCK), 0) << ((slot & 3) * 8)
        number[4] = pos & (BLOCK - 1)
        for q in range(4):
            number[q] = jnp.where((slot >> 2) == q, value, 0)
        side = block // pairs
        for at in range(0, BLOCK, tile):
            here = at + lax.broadcasted_iota(jnp.int32, (tile, BLOCK), 0)
            acc = [jnp.full((tile, BLOCK), 0x40404040 * side, jnp.int32) for _ in range(4)]
            for n in range(1, neighbours + 1):
                hit = jnp.broadcast_to(number[4, n : n + 1, :], (tile, BLOCK)) == here
                for q in range(4):
                    word = jnp.broadcast_to(number[q, n : n + 1, :], (tile, BLOCK))
                    acc[q] = acc[q] | jnp.where(hit, word, 0)
            for q in range(4):
                turned[q, at : at + tile, :] = acc[q]
        rows = pl.ds(pl.multiple_of((block - side * pairs) * BLOCK, BLOCK), BLOCK)
        for q in range(4):
            code[side * 4 + q, rows, :] = turned[q].T
        return 0

    early = blocks // 3
    late = blocks - 2
    lax.fori_loop(0, early, encode, 0)
    emb_gather.forward_first()
    lax.fori_loop(early, late, encode, 0)
    emb_gather.forward_rest()
    lab_gather.start()
    emb_gather.finish()

    lower = lax.broadcasted_iota(jnp.int32, (BLOCK, LANES), 1) < HALF

    def score(b, _):
        rows = pl.ds(pl.multiple_of(b * BLOCK, BLOCK), BLOCK)
        pos = pos_ref[rows, :]
        inside = pos & (BLOCK - 1)
        slot = pos >> 7
        acc = jnp.zeros((BLOCK, LANES), jnp.float32)
        for k in range(0, SLOTS, 2):
            picked = [None, None]
            for h in range(2):
                block = b + h * pairs
                q_rows = pl.ds(pl.multiple_of(block * BLOCK, BLOCK), BLOCK)
                cand = jnp.concatenate(
                    [emb_all[pattern_ref[block, k]], emb_all[pattern_ref[block, k + 1]]], axis=1
                )
                picked[h] = jnp.dot(query_ref[q_rows, :], cand, preferred_element_type=jnp.float32)
            for u in range(2):
                cols = slice(u * LANES, (u + 1) * LANES)
                got = jnp.where(
                    lower, lane_pick(picked[0][:, cols], inside), lane_pick(picked[1][:, cols], inside)
                )
                acc = jnp.where(slot == k + u, got, acc)
        part[rows, :] = acc
        return 0

    lax.fori_loop(0, pairs, score, 0)

    rs_copies = [
        pltpu.make_async_remote_copy(
            src_ref=part.at[pl.ds(row_peer(d) * chunk, chunk)],
            dst_ref=rs_buf.at[d],
            send_sem=rs_send.at[d],
            recv_sem=rs_recv.at[d],
            device_id=(row_peer(d), me_col),
            device_id_type=MESH,
        )
        for d in range(1, n_row)
    ]
    for copy in rs_copies:
        copy.start()
    lab_gather.forward_first()
    lax.fori_loop(late, late + 1, encode, 0)
    my_rows = pl.ds(pl.multiple_of(me_row * chunk, chunk), chunk)
    total = part[my_rows, :]
    for d, copy in enumerate(rs_copies):
        copy.wait()
        total = total + rs_buf[d + 1]

    low = lax.broadcasted_iota(jnp.int32, (chunk, LANES), 1) < HALF
    valid = pos_ref[my_rows, :] >= 0
    logits = jnp.where(valid, total / math.sqrt(width) * sharp_ref[my_rows, :], lowest_logit)

    def by_half(reduce, values, neutral):
        first = reduce(jnp.where(low, values, neutral), axis=1, keepdims=True)
        second = reduce(jnp.where(low, neutral, values), axis=1, keepdims=True)
        return jnp.where(low, first, second)

    top = by_half(jnp.max, logits, lowest_logit)
    expo = jnp.where(valid, jnp.exp(logits - top), 0.0)
    sums = by_half(jnp.sum, expo, 0.0)
    w_all[my_rows, :] = (expo / sums).astype(jnp.bfloat16)

    w_copies = [
        pltpu.make_async_remote_copy(
            src_ref=w_all.at[my_rows],
            dst_ref=w_all.at[my_rows],
            send_sem=w_send.at[d],
            recv_sem=w_recv.at[d],
            device_id=(row_peer(d), me_col),
            device_id_type=MESH,
        )
        for d in range(1, n_row)
    ]
    for copy in w_copies:
        copy.start()
    lax.fori_loop(late + 1, blocks, encode, 0)
    lab_gather.forward_rest()
    for copy in w_copies:
        copy.wait()
    lab_gather.finish()

    def blend(acc, block):
        return (mixing * acc + (1.0 - mixing) * lab_ref[block].astype(jnp.float32)).astype(
            jnp.bfloat16
        )

    def first_round(h, b, _):
        rows = pl.ds(pl.multiple_of(b * BLOCK, BLOCK), BLOCK)
        weights = w_all[rows, :].astype(jnp.float32)
        block = b + h * pairs
        acc = jnp.zeros((BLOCK, classes), jnp.float32)
        for k in range(0, SLOTS, 2):
            pieces = []
            for u in range(k, k + 2):
                index = (code[h * 4 + u // 4, rows, :] >> (8 * (u % 4))) & 0x7F
                pieces.append(lane_pick(weights, index).astype(jnp.bfloat16))
            wide = jnp.concatenate(pieces, axis=1)
            dense[block, :, k * BLOCK : (k + 2) * BLOCK] = wide
            cand = jnp.concatenate(
                [lab_all[pattern_ref[block, k]], lab_all[pattern_ref[block, k + 1]]], axis=0
            )
            acc += jnp.dot(wide, cand, preferred_element_type=jnp.float32)
        spread_all[me_col * blocks + block] = blend(acc, block)
        return 0

    for h in range(2):
        lax.fori_loop(0, pairs, functools.partial(first_round, h), 0)
        spread_gather.start_half(h)
    spread_gather.forward_first()
    spread_gather.forward_rest()
    spread_gather.finish()

    def second_round(block, _):
        acc = jnp.zeros((BLOCK, classes), jnp.float32)
        for k in range(0, SLOTS, 2):
            cand = jnp.concatenate(
                [spread_all[pattern_ref[block, k]], spread_all[pattern_ref[block, k + 1]]], axis=0
            )
            acc += jnp.dot(
                dense[block, :, k * BLOCK : (k + 2) * BLOCK], cand, preferred_element_type=jnp.float32
            )
        out_ref[block] = blend(acc, block)
        return 0

    lax.fori_loop(0, blocks, second_round, 0)


def body(embeds, labels, sharpness, pattern, mask_pos):
    rows_here, width = embeds.shape
    classes = labels.shape[1]
    neighbours = mask_pos.shape[1]
    n_col = lax.axis_size("col")
    n_row = lax.axis_size("row")
    row_pos = lax.axis_index("row")
    blocks = rows_here // BLOCK
    packed = rows_here // 2
    features = width // n_row
    per_device = classes // n_row
    wide = -(-per_device // LANES) * LANES

    query = lax.dynamic_slice_in_dim(embeds, row_pos * features, features, 1)
    emb = query.reshape(blocks, BLOCK, features).transpose(0, 2, 1)
    lab = lax.dynamic_slice_in_dim(labels, row_pos * per_device, per_device, 1)
    lab = jnp.pad(lab, ((0, 0), (0, wide - per_device))).reshape(blocks, BLOCK, wide)
    pos = jnp.pad(mask_pos, ((0, 0), (1, HALF - 1 - neighbours)), constant_values=-1)
    post = pos.T
    sharpt = sharpness.reshape(1, rows_here)
    total_blocks = n_col * blocks
    vmem = pl.BlockSpec(memory_space=pltpu.VMEM)
    out = pl.pallas_call(
        functools.partial(kernel, n_row, n_col, neighbours, width),
        out_shape=jax.ShapeDtypeStruct((blocks, BLOCK, wide), jnp.bfloat16),
        in_specs=[pl.BlockSpec(memory_space=pltpu.SMEM)] + [vmem] * 5,
        out_specs=vmem,
        scratch_shapes=[
            pltpu.VMEM((packed, LANES), jnp.int32),
            pltpu.VMEM((packed, LANES), jnp.float32),
            pltpu.VMEM((total_blocks, features, BLOCK), jnp.bfloat16),
            pltpu.VMEM((total_blocks, BLOCK, wide), jnp.bfloat16),
            pltpu.VMEM((total_blocks, BLOCK, wide), jnp.bfloat16),
            pltpu.VMEM((8, packed, LANES), jnp.int32),
            pltpu.VMEM((4, BLOCK, BLOCK), jnp.int32),
            pltpu.VMEM((5, HALF, BLOCK), jnp.int32),
            pltpu.VMEM((packed, LANES), jnp.float32),
            pltpu.VMEM((n_row, packed // n_row, LANES), jnp.float32),
            pltpu.VMEM((packed, LANES), jnp.bfloat16),
            pltpu.VMEM((blocks, BLOCK, SLOTS * BLOCK), jnp.bfloat16),
            pltpu.SemaphoreType.DMA((2,)),
        ]
        + [pltpu.SemaphoreType.DMA((max(n_col, 14),))] * 6
        + [pltpu.SemaphoreType.DMA((n_row,))] * 4,
        compiler_params=pltpu.CompilerParams(
            collective_id=0, has_side_effects=True, vmem_limit_bytes=48 * 1024 * 1024
        ),
    )(pattern, query, emb, lab, post, sharpt)
    return out.reshape(rows_here, wide)[:, :per_device]


def solution(mesh):
    placed = (P("col", None), P("col", None), P("col"), P("col", None), P("col", None))
    return jax.shard_map(
        body, mesh=mesh, in_specs=placed, out_specs=P("col", "row"), check_vma=False
    )
```
